1024 devices in a mesh: doc: 64 (over y_hi, z), label: 16 (over x, y_lo, core).
Axes of the slice: x: 4, y: 4 (y_hi: 2, y_lo: 2; y = y_hi * 2 + y_lo), z: 32, core: 2. Of those that a mesh axis runs over, the one named last changes fastest.
Arguments:
- doc_emb: bfloat16 [65536, 768], P(('doc', 'label'))
- label_emb: bfloat16 [16384, 768], P(('label', 'doc'))
- short_blocks: int32 [256, 32], replicated, may hold values from 0 to 127, as said below
- short_len: int32 [256], replicated, may hold values from 1 to 32, as said below
- positives: int32 [65536, 8], P('doc'), may hold values from 0 to 16383, as said below
Outputs:
- doc_grad: float32 [65536, 768], P(('doc', 'label'))
The draws below stay inside these ranges and needn't reach their ends.
Inputs may be any that keep to these rules, and one draw needn't show every extreme that they name: `short_blocks`: each row lists, in a random order, 2 distinct blocks out of every run of 8 consecutive label blocks k * 8 to (k + 1) * 8 - 1. `short_len`: some row is full. `positives`: every positive of a document lies in a label block among the live entries of its block's list; ids may repeat.
All inputs are finite; a program needn't handle non-finite values.
Results may differ from the reference program's by a relative error of at most 0.0045.
Values may be sent and summed in bfloat16 or wider, within the bound.
No kernel may reach another device: no remote copies, remote signals or barrier semaphores. Data moves between devices by JAX's collectives and lax.ppermute only.
A program may use at most 32 MiB of HBM per device.

```python
import math
import jax
import jax.numpy as jnp
from jax import lax

D = 768
DOC_BLK = 256
LAB_BLK = 128
POS = 8
DOCS = 65536
LABELS = 16384
LBLKS = 128
DBLKS = 256
SHARD_BLK = 8
CAP = 2
SLOTS = 32


def embed_rows(key, row_count, salt):
    key_entries = jax.random.fold_in(key, salt)
    key_scales = jax.random.fold_in(key, salt + 1)
    entries = jax.random.normal(key_entries, (row_count, D), jnp.float32)
    row_scale = jnp.exp(jax.random.uniform(key_scales, (row_count, 1), jnp.float32, math.log(3.0), math.log(30.0)))
    return (entries * row_scale / math.sqrt(D)).astype(jnp.bfloat16)


def draw_doc_emb(key, part):
    return embed_rows(key, DOCS, 11)


def draw_label_emb(key, part):
    return embed_rows(key, LABELS, 21)


def shortlist_parts(key):
    shard_count = SLOTS // CAP
    raw_bits = jax.random.randint(jax.random.fold_in(key, 31), (DBLKS, shard_count, SHARD_BLK), 0, 1 << 20)
    ranked = raw_bits * SHARD_BLK + jnp.arange(SHARD_BLK, dtype=jnp.int32)
    local_ids = jnp.argsort(ranked, axis=-1)[..., :CAP].astype(jnp.int32)
    block_ids = local_ids + (jnp.arange(shard_count, dtype=jnp.int32) * SHARD_BLK)[None, :, None]
    block_ids = block_ids.reshape(DBLKS, SLOTS)
    shuffle_bits = jax.random.randint(jax.random.fold_in(key, 32), (DBLKS, SLOTS), 0, 1 << 20)
    shuffle = jnp.argsort(shuffle_bits * SLOTS + jnp.arange(SLOTS, dtype=jnp.int32), axis=-1)
    block_ids = jnp.take_along_axis(block_ids, shuffle, axis=-1).astype(jnp.int32)
    list_len = jax.random.randint(jax.random.fold_in(key, 33), (DBLKS,), 1, SLOTS + 1)
    full_row = jax.random.randint(jax.random.fold_in(key, 34), (), 0, DBLKS)
    list_len = jnp.where(jnp.arange(DBLKS, dtype=jnp.int32) == full_row, SLOTS, list_len).astype(jnp.int32)
    return (block_ids, list_len)


def draw_short_blocks(key, part):
    return shortlist_parts(key)[0]


def draw_short_len(key, part):
    return shortlist_parts(key)[1]


def draw_positives(key, part):
    block_ids, list_len = shortlist_parts(key)
    owner_block = jnp.arange(DOCS, dtype=jnp.int32) // DOC_BLK
    slot_bits = jax.random.randint(jax.random.fold_in(key, 41), (DOCS, POS), 0, 1 << 20)
    slot_pick = slot_bits % list_len[owner_block][:, None]
    chosen = jnp.take_along_axis(block_ids[owner_block], slot_pick, axis=1)
    offsets = jax.random.randint(jax.random.fold_in(key, 42), (DOCS, POS), 0, LAB_BLK)
    return (chosen * LAB_BLK + offsets).astype(jnp.int32)


def setup_inputs(seed: int = 0) -> dict:
    streams_of = jax.random.split(jax.random.key(seed), 6)
    doc_emb = draw_doc_emb(jax.random.fold_in(streams_of[5], 71), 0)
    label_emb = draw_label_emb(jax.random.fold_in(streams_of[5], 71), 0)
    short_blocks = draw_short_blocks(jax.random.fold_in(streams_of[5], 71), 0)
    short_len = draw_short_len(jax.random.fold_in(streams_of[5], 71), 0)
    positives = draw_positives(jax.random.fold_in(streams_of[5], 71), 0)
    return dict(doc_emb=doc_emb, label_emb=label_emb, short_blocks=short_blocks, short_len=short_len, positives=positives)


SCALE = 16.0

def unit_rows(matrix):
    widened = matrix.astype(jnp.float32)
    row_norm = jnp.sqrt(lax.optimization_barrier(jnp.sum(widened * widened, axis=-1, keepdims=True)) + 1e-06)
    return (widened / row_norm, row_norm)

def reference(doc_emb, label_emb, short_blocks, short_len, positives):
    doc_unit, doc_norm = unit_rows(doc_emb)
    doc_half = doc_unit.astype(jnp.bfloat16)
    label_unit, _ = unit_rows(label_emb)
    label_half = label_unit.astype(jnp.bfloat16).reshape(LBLKS, LAB_BLK, D)
    doc_blocks = doc_half.reshape(DBLKS, DOC_BLK, D)
    pos_blocks = positives.reshape(DBLKS, DOC_BLK, POS)

    def one_block(block_args):
        block_docs, block_ids, list_len, block_pos = block_args
        panels = label_half[block_ids].astype(jnp.float32)
        scores = SCALE * jnp.einsum('dk,tlk->dtl', block_docs.astype(jnp.float32), panels, precision=lax.Precision.HIGHEST)
        labels = block_ids[:, None] * LAB_BLK + jnp.arange(LAB_BLK, dtype=jnp.int32)[None, :]
        hit_count = jnp.zeros(scores.shape, jnp.float32)
        for column in range(POS):
            hit_count = hit_count + (block_pos[:, column][:, None, None] == labels[None, :, :]).astype(jnp.float32)
        target = jnp.minimum(hit_count, 1.0)
        live_slots = (jnp.arange(SLOTS, dtype=jnp.int32) < list_len).astype(jnp.float32)
        pair_coef = (SCALE * (jax.nn.sigmoid(scores) - target) * live_slots[None, :, None]).astype(jnp.bfloat16)
        return jnp.einsum('dtl,tlk->dk', pair_coef.astype(jnp.float32), panels, precision=lax.Precision.HIGHEST)
    doc_push = lax.map(one_block, (doc_blocks, short_blocks, short_len, pos_blocks)).reshape(DOCS, D)
    radial = lax.optimization_barrier(jnp.sum(doc_push * doc_unit, axis=-1, keepdims=True))
    return (doc_push - radial * doc_unit) / doc_norm
```

```python
import jax
import jax.numpy as jnp
from jax import lax
from jax.sharding import Mesh, PartitionSpec as P

DOC_BLK = 256
LAB_BLK = 128
POS = 8
SCALE = 16.0

AXES = ("yh", "zp", "zb", "x", "yl", "c")
SIZES = (2, 16, 2, 4, 2, 2)
PLANE = ("yh", "x", "yl")


def unit_rows(matrix):
    widened = matrix.astype(jnp.float32)
    row_norm = jnp.sqrt(jnp.sum(widened * widened, axis=-1, keepdims=True) + 1e-06)
    return widened / row_norm, row_norm


def body(doc_emb, label_emb, short_blocks, short_len, positives):
    rows, width = doc_emb.shape
    yh, x, yl, core = (lax.axis_index(a) for a in ("yh", "x", "yl", "c"))
    depth = lax.axis_index(("zp", "zb"))
    plane = 16

    label_half = unit_rows(label_emb)[0].astype(jnp.bfloat16)
    pair = lax.all_gather(label_half, "zb", axis=0, tiled=True)

    own_unit, own_norm = unit_rows(doc_emb)
    own_pos = lax.dynamic_slice_in_dim(positives, ((x * 2 + yl) * 2 + core) * rows, rows, 0)
    packed = jnp.concatenate(
        [
            own_unit.astype(jnp.bfloat16),
            (own_pos // LAB_BLK).astype(jnp.bfloat16),
            (own_pos % LAB_BLK).astype(jnp.bfloat16),
            jnp.zeros((rows, 128 - 2 * POS), jnp.bfloat16),
        ],
        axis=1,
    )
    spread = jnp.broadcast_to(packed[None], (plane,) + packed.shape)
    docs = lax.all_to_all(spread, PLANE, split_axis=0, concat_axis=0, tiled=True)
    docs = docs.reshape(plane * rows, -1)

    own_labels = lax.all_gather(pair, "zp", axis=0, tiled=True)
    other_labels = lax.ppermute(own_labels, "c", [(0, 1), (1, 0)])
    labels = jnp.concatenate([own_labels, other_labels], axis=0)
    half = own_labels.shape[0]

    shard = (x * 2 + yl) * 2 + core
    first_own = shard * 8 + yh * 4
    first_other = (shard + 1 - 2 * core) * 8 + yh * 4
    grid = jnp.arange(4, dtype=jnp.int32)
    block_ids = jnp.concatenate([first_own + grid, first_other + grid])
    label_ids = (block_ids[:, None] * LAB_BLK + jnp.arange(LAB_BLK, dtype=jnp.int32)).reshape(-1)

    listed = short_blocks.reshape(2, 32, 4, 32)
    listed = lax.dynamic_index_in_dim(listed, depth, 1, keepdims=False).reshape(8, 32)
    list_len = lax.dynamic_index_in_dim(short_len.reshape(2, 32, 4), depth, 1, keepdims=False)
    list_len = list_len.reshape(8)
    in_list = jnp.arange(32, dtype=jnp.int32)[None, :] < list_len[:, None]
    active = jnp.any(
        (listed[:, :, None] == block_ids[None, None, :]) & in_list[:, :, None], axis=1
    ).astype(jnp.float32)

    doc_half = docs[:, :width]
    places = docs[:, width : width + 2 * POS].astype(jnp.float32)
    pos_ids = (places[:, :POS] * LAB_BLK + places[:, POS:]).astype(jnp.int32)
    scores = SCALE * lax.dot_general(
        doc_half, labels, (((1,), (1,)), ((), ())), preferred_element_type=jnp.float32
    )
    hit = jnp.zeros(scores.shape, jnp.bool_)
    for column in range(POS):
        hit = hit | (pos_ids[:, column][:, None] == label_ids[None, :])
    coef = SCALE * (jax.nn.sigmoid(scores) - hit.astype(jnp.float32))
    coef = (coef.reshape(8, 128, 8, LAB_BLK) * active[:, None, :, None]).reshape(1024, 1024)
    push = jnp.dot(coef.astype(jnp.bfloat16), labels, preferred_element_type=jnp.float32)
    pieces = lax.all_to_all(
        push.astype(jnp.bfloat16).reshape(plane, rows, width),
        PLANE,
        split_axis=0,
        concat_axis=0,
        tiled=True,
    )
    summed = jnp.sum(pieces.astype(jnp.float32), axis=0)
    radial = jnp.sum(summed * own_unit, axis=-1, keepdims=True)
    return (summed - radial * own_unit) / own_norm


def solution(mesh):
    fine = Mesh(mesh.devices.reshape(SIZES), AXES)
    doc, label = AXES[:3], AXES[3:]
    placed = (P(doc + label, None), P(label + doc, None), P(), P(), P(doc, None))
    return jax.shard_map(
        body, mesh=fine, in_specs=placed, out_specs=P(doc + label, None), check_vma=False
    )
```

```python
import jax
import jax.numpy as jnp
from jax import lax
from jax.experimental import pallas as pl
from jax.experimental.pallas import tpu as pltpu
from jax.sharding import Mesh, PartitionSpec as P

DOC_BLK = 256
LAB_BLK = 128
POS = 8
SCALE = 16.0

AXES = ("yh", "zp", "zb", "x", "yl", "c")
SIZES = (2, 16, 2, 4, 2, 2)
PLANE = ("yh", "x", "yl")


def unit_rows(matrix):
    widened = matrix.astype(jnp.float32)
    row_norm = jnp.sqrt(jnp.sum(widened * widened, axis=-1, keepdims=True) + 1e-06)
    return widened / row_norm, row_norm


def push_kernel(live_ref, docs_ref, own_ref, other_ref, out_ref, total):
    yh, x, yl, core = (lax.axis_index(a) for a in ("yh", "x", "yl", "c"))
    depth = lax.axis_index("zp") * 2 + lax.axis_index("zb")
    width = own_ref.shape[1]
    shard = (x * 2 + yl) * 2 + core
    firsts = (shard * 8 + yh * 4, (shard + 1 - 2 * core) * 8 + yh * 4)
    lane = lax.broadcasted_iota(jnp.int32, (1, 2 * LAB_BLK), 1)
    upper = lane >= LAB_BLK

    @pl.loop(0, 8)
    def _(run):
        rows = pl.ds(pl.multiple_of(run * 128, 128), 128)
        column = (run // 4) * 128 + depth * 4 + run % 4
        total[...] = jnp.zeros_like(total)
        for side, labels_ref in ((0, own_ref), (1, other_ref)):
            live = [live_ref[side * 4 + i, column] for i in range(4)]
            count = live[0] + live[1] + live[2] + live[3]
            low = jnp.where(live[0] > 0, 0, jnp.where(live[1] > 0, 1, jnp.where(live[2] > 0, 2, 3)))
            high = jnp.where(live[3] > 0, 3, jnp.where(live[2] > 0, 2, jnp.where(live[1] > 0, 1, 0)))

            @pl.when(count > 0)
            def _():
                panel = jnp.concatenate(
                    [
                        labels_ref[pl.ds(pl.multiple_of(b * LAB_BLK, LAB_BLK), LAB_BLK), :]
                        for b in (low, high)
                    ],
                    axis=0,
                )
                scores = SCALE * lax.dot_general(
                    docs_ref[rows, :width],
                    panel,
                    (((1,), (1,)), ((), ())),
                    preferred_element_type=jnp.float32,
                )
                places = docs_ref[rows, width:].astype(jnp.float32)
                pos_ids = places[:, :POS] * LAB_BLK + places[:, POS : 2 * POS]
                ids = (firsts[side] + jnp.where(upper, high - 1, low)) * LAB_BLK + lane
                ids = ids.astype(jnp.float32)
                hit = pos_ids[:, 0:1] == ids
                for k in range(1, POS):
                    hit = hit | (pos_ids[:, k : k + 1] == ids)
                coef = SCALE * (jax.nn.sigmoid(scores) - jnp.where(hit, 1.0, 0.0))
                coef = jnp.where(upper & (count < 2), 0.0, coef)
                total[...] += jnp.dot(
                    coef.astype(jnp.bfloat16), panel, preferred_element_type=jnp.float32
                )

        out_ref[rows, :] = total[...].astype(jnp.bfloat16)


def body(doc_emb, label_emb, short_blocks, short_len, positives):
    rows, width = doc_emb.shape
    yh, x, yl, core = (lax.axis_index(a) for a in ("yh", "x", "yl", "c"))
    plane = 16

    label_half = unit_rows(label_emb)[0].astype(jnp.bfloat16)
    pair = lax.all_gather(label_half, "zb", axis=0, tiled=True)

    own_unit, own_norm = unit_rows(doc_emb)
    own_pos = lax.dynamic_slice_in_dim(positives, ((x * 2 + yl) * 2 + core) * rows, rows, 0)
    packed = jnp.concatenate(
        [
            own_unit.astype(jnp.bfloat16),
            (own_pos // LAB_BLK).astype(jnp.bfloat16),
            (own_pos % LAB_BLK).astype(jnp.bfloat16),
            jnp.zeros((rows, 128 - 2 * POS), jnp.bfloat16),
        ],
        axis=1,
    )
    spread = jnp.broadcast_to(packed[None], (plane,) + packed.shape)
    docs = lax.all_to_all(spread, PLANE, split_axis=0, concat_axis=0, tiled=True)
    docs = docs.reshape(plane * rows, -1)

    own_labels = lax.all_gather(pair, "zp", axis=0, tiled=True)
    other_labels = lax.ppermute(own_labels, "c", [(0, 1), (1, 0)])

    shard = (x * 2 + yl) * 2 + core
    grid = jnp.arange(4, dtype=jnp.int32)
    block_ids = yh * 4 + jnp.concatenate([shard * 8 + grid, (shard + 1 - 2 * core) * 8 + grid])
    slot = jnp.arange(short_blocks.shape[1], dtype=jnp.int32)
    live = jnp.any(
        (short_blocks.T[None] == block_ids[:, None, None])
        & (slot[:, None] < short_len[None, :])[None],
        axis=1,
    ).astype(jnp.int32)

    push = pl.pallas_call(
        push_kernel,
        out_shape=jax.ShapeDtypeStruct((plane * rows, width), jnp.bfloat16),
        in_specs=[pl.BlockSpec(memory_space=pltpu.SMEM)]
        + [pl.BlockSpec(memory_space=pltpu.VMEM)] * 3,
        out_specs=pl.BlockSpec(memory_space=pltpu.VMEM),
        scratch_shapes=[pltpu.VMEM((128, width), jnp.float32)],
        compiler_params=pltpu.CompilerParams(vmem_limit_bytes=32 * 2**20),
    )(live, docs, own_labels, other_labels)
    pieces = lax.all_to_all(
        push.reshape(plane, rows, width),
        PLANE,
        split_axis=0,
        concat_axis=0,
        tiled=True,
    )
    summed = jnp.sum(pieces.astype(jnp.float32), axis=0)
    radial = jnp.sum(summed * own_unit, axis=-1, keepdims=True)
    return (summed - radial * own_unit) / own_norm


def solution(mesh):
    fine = Mesh(mesh.devices.reshape(SIZES), AXES)
    doc, label = AXES[:3], AXES[3:]
    placed = (P(doc + label, None), P(label + doc, None), P(), P(), P(doc, None))
    return jax.shard_map(
        body, mesh=fine, in_specs=placed, out_specs=P(doc + label, None), check_vma=False
    )
```

```python
import functools

import jax
import jax.numpy as jnp
from jax import lax
from jax.experimental import pallas as pl
from jax.experimental.pallas import tpu as pltpu
from jax.sharding import Mesh, PartitionSpec as P

LAB_BLK = 128
POS = 8
SCALE = 16.0
RUN = 128
RUNS = 8

AXES = ("yh", "zp", "zb", "x", "yl", "c")
SIZES = (2, 16, 2, 4, 2, 2)
PLANE = ("yh", "x", "yl")
PLANE_SIZE = 16


def unit_rows(matrix):
    widened = matrix.astype(jnp.float32)
    row_norm = jnp.sqrt(jnp.sum(widened * widened, axis=-1, keepdims=True) + 1e-06)
    return widened / row_norm, row_norm


def place():
    return tuple(lax.axis_index(a) for a in AXES)


def first_blocks():
    yh, _, _, x, yl, core = place()
    shard = (x * 2 + yl) * 2 + core
    return shard * 8 + yh * 4, (shard + 1 - 2 * core) * 8 + yh * 4


def prepare_kernel(doc_ref, label_ref, pos_ref, half_ref, spread_ref, packed, sems):
    half_ref[...] = unit_rows(label_ref[...])[0].astype(jnp.bfloat16)
    rows, width = doc_ref.shape
    packed[:, :width] = unit_rows(doc_ref[...])[0].astype(jnp.bfloat16)
    _, _, _, x, yl, core = place()
    ids = pos_ref[:, pl.ds(pl.multiple_of((x * 2 + yl) * 128, 128), 128)]
    parts = jnp.concatenate(
        [
            (ids // LAB_BLK).astype(jnp.float32),
            (ids % LAB_BLK).astype(jnp.float32),
            jnp.zeros((128 - 2 * POS, 128), jnp.float32),
        ],
        axis=0,
    )
    parts = parts.T
    packed[:, width:] = jnp.where(core == 0, parts[:rows], parts[rows:]).astype(jnp.bfloat16)
    copies = [
        pltpu.make_async_copy(packed, spread_ref.at[i], sems.at[i]) for i in range(PLANE_SIZE)
    ]
    for copy in copies:
        copy.start()
    for copy in copies:
        copy.wait()


def push_kernel(side, live_ref, docs_ref, labels_ref, *refs):
    before_ref, out_ref, tasks = refs if side else (None, *refs)
    _, zp, zb, _, _, _ = place()
    width = labels_ref.shape[1]
    first = first_blocks()[side]
    lane = lax.broadcasted_iota(jnp.int32, (1, 2 * LAB_BLK), 1)
    upper = lane >= LAB_BLK
    offset = (lane % LAB_BLK) ^ (16 * zb)

    number = jnp.int32(0)
    for run in range(RUNS):
        column = (run // 4) * 128 + (zp * 2 + zb) * 4 + run % 4
        live = [live_ref[side * 4 + i, column] for i in range(4)]
        count = live[0] + live[1] + live[2] + live[3]
        low = jnp.where(live[0] > 0, 0, jnp.where(live[1] > 0, 1, jnp.where(live[2] > 0, 2, 3)))
        high = jnp.where(live[3] > 0, 3, jnp.where(live[2] > 0, 2, jnp.where(live[1] > 0, 1, 0)))
        tasks[4 * number] = run
        tasks[4 * number + 1] = low
        tasks[4 * number + 2] = high
        tasks[4 * number + 3] = count
        number = number + jnp.where(count > 0, 1, 0)

        @pl.when(count == 0)
        def _():
            rows = pl.ds(run * RUN, RUN)
            if side:
                out_ref[rows, :] = before_ref[rows, :].astype(out_ref.dtype)
            else:
                out_ref[rows, :] = jnp.zeros((RUN, width), out_ref.dtype)

    def work(task):
        run, low, high, count = (tasks[4 * task + i] for i in range(4))
        rows = pl.ds(pl.multiple_of(run * RUN, RUN), RUN)
        panel = jnp.concatenate(
            [
                labels_ref[pl.ds(pl.multiple_of(b * LAB_BLK, LAB_BLK), LAB_BLK), :]
                for b in (low, high)
            ],
            axis=0,
        )
        scores = SCALE * lax.dot_general(
            docs_ref[rows, :width],
            panel,
            (((1,), (1,)), ((), ())),
            preferred_element_type=jnp.float32,
        )
        places = docs_ref[rows, width:].astype(jnp.float32)
        pos_ids = places[:, :POS] * LAB_BLK + places[:, POS : 2 * POS]
        ids = ((first + jnp.where(upper, high, low)) * LAB_BLK + offset).astype(jnp.float32)
        hit = pos_ids[:, 0:1] == ids
        for k in range(1, POS):
            hit = hit | (pos_ids[:, k : k + 1] == ids)
        coef = SCALE * (jax.nn.sigmoid(scores) - jnp.where(hit, 1.0, 0.0))
        coef = jnp.where(upper & (count < 2), 0.0, coef).astype(jnp.bfloat16)
        total = jnp.dot(coef, panel, preferred_element_type=jnp.float32)
        if side:
            total = total + before_ref[rows, :]
        return rows, total.astype(out_ref.dtype)

    @pl.loop(0, (number + 1) // 2)
    def _(pair):
        results = [work(2 * pair), work(jnp.minimum(2 * pair + 1, number - 1))]
        for rows, total in results:
            out_ref[rows, :] = total


def vmem(count):
    return [pl.BlockSpec(memory_space=pltpu.VMEM)] * count


def body(doc_emb, label_emb, short_blocks, short_len, positives):
    rows, width = doc_emb.shape
    label_half, spread = pl.pallas_call(
        prepare_kernel,
        out_shape=(
            jax.ShapeDtypeStruct(label_emb.shape, jnp.bfloat16),
            jax.ShapeDtypeStruct((PLANE_SIZE, rows, width + 128), jnp.bfloat16),
        ),
        in_specs=vmem(3),
        out_specs=(vmem(1)[0], pl.BlockSpec(memory_space=pl.ANY)),
        scratch_shapes=[
            pltpu.VMEM((rows, width + 128), jnp.bfloat16),
            pltpu.SemaphoreType.DMA((PLANE_SIZE,)),
        ],
    )(doc_emb, label_emb, positives.T)

    neighbour = lax.ppermute(label_half, "zb", [(0, 1), (1, 0)])
    docs = lax.all_to_all(spread, PLANE, split_axis=0, concat_axis=0, tiled=True)
    docs = docs.reshape(PLANE_SIZE * rows, width + 128)
    pair = jnp.concatenate([label_half, neighbour], axis=0)
    own_labels = lax.all_gather(pair, "zp", axis=0, tiled=True)
    other_labels = lax.ppermute(own_labels, "c", [(0, 1), (1, 0)])

    grid = jnp.arange(4, dtype=jnp.int32)
    block_ids = jnp.concatenate([first + grid for first in first_blocks()])
    slot = jnp.arange(short_blocks.shape[1], dtype=jnp.int32)
    live = jnp.any(
        (short_blocks.T[None] == block_ids[:, None, None])
        & (slot[:, None] < short_len[None, :])[None],
        axis=1,
    ).astype(jnp.int32)

    def push(side, dtype, *operands):
        return pl.pallas_call(
            functools.partial(push_kernel, side),
            out_shape=jax.ShapeDtypeStruct((RUNS * RUN, width), dtype),
            in_specs=[pl.BlockSpec(memory_space=pltpu.SMEM)] + vmem(len(operands)),
            out_specs=vmem(1)[0],
            scratch_shapes=[pltpu.SMEM((4 * RUNS + 4,), jnp.int32)],
            compiler_params=pltpu.CompilerParams(vmem_limit_bytes=32 * 2**20),
            cost_estimate=pl.CostEstimate(
                flops=4 * RUNS * RUN * 2 * LAB_BLK * width,
                bytes_accessed=6 * 2**20,
                transcendentals=2 * RUNS * RUN * 2 * LAB_BLK,
            ),
        )(live, *operands)

    part = push(0, jnp.float32, docs, own_labels)
    part = push(1, jnp.bfloat16, docs, other_labels, part)
    pieces = lax.all_to_all(
        part.reshape(PLANE_SIZE, rows, width), PLANE, split_axis=0, concat_axis=0, tiled=True
    )
    own_unit, own_norm = unit_rows(doc_emb)
    summed = jnp.sum(pieces.astype(jnp.float32), axis=0)
    radial = jnp.sum(summed * own_unit, axis=-1, keepdims=True)
    return (summed - radial * own_unit) / own_norm


def solution(mesh):
    fine = Mesh(mesh.devices.reshape(SIZES), AXES)
    doc, label = AXES[:3], AXES[3:]
    placed = (P(doc + label, None), P(label + doc, None), P(), P(), P(doc, None))
    return jax.shard_map(
        body, mesh=fine, in_specs=placed, out_specs=P(doc + label, None), check_vma=False
    )
```

```python
import functools

import jax
import jax.numpy as jnp
from jax import lax
from jax.experimental import pallas as pl
from jax.experimental.pallas import tpu as pltpu
from jax.sharding import Mesh, PartitionSpec as P

LAB_BLK = 128
POS = 8
SCALE = 16.0
RUN = 128
RUNS = 8

AXES = ("yh", "zp", "zb", "x", "yl", "c")
SIZES = (2, 16, 2, 4, 2, 2)
PLANE = ("yh", "x", "yl")
PLANE_SIZE = 16


def unit_rows(matrix):
    widened = matrix.astype(jnp.float32)
    row_norm = jnp.sqrt(jnp.sum(widened * widened, axis=-1, keepdims=True) + 1e-06)
    return widened / row_norm, row_norm


def place():
    return tuple(lax.axis_index(a) for a in AXES)


def first_blocks():
    yh, _, _, x, yl, core = place()
    shard = (x * 2 + yl) * 2 + core
    return shard * 8 + yh * 4, (shard + 1 - 2 * core) * 8 + yh * 4


def prepare_kernel(doc_ref, label_ref, pos_ref, half_ref, spread_ref, packed, sems):
    half_ref[...] = unit_rows(label_ref[...])[0].astype(jnp.bfloat16)
    rows, width = doc_ref.shape
    packed[:, :width] = unit_rows(doc_ref[...])[0].astype(jnp.bfloat16)
    _, _, _, x, yl, core = place()
    ids = pos_ref[:, pl.ds(pl.multiple_of((x * 2 + yl) * 128, 128), 128)]
    parts = jnp.concatenate(
        [
            (ids // LAB_BLK).astype(jnp.float32),
            (ids % LAB_BLK).astype(jnp.float32),
            jnp.zeros((128 - 2 * POS, 128), jnp.float32),
        ],
        axis=0,
    )
    parts = parts.T
    packed[:, width:] = jnp.where(core == 0, parts[:rows], parts[rows:]).astype(jnp.bfloat16)
    copies = [
        pltpu.make_async_copy(packed, spread_ref.at[i], sems.at[i]) for i in range(PLANE_SIZE)
    ]
    for copy in copies:
        copy.start()
    for copy in copies:
        copy.wait()


def push_kernel(side, live_ref, docs_ref, labels_ref, *refs):
    before_ref, out_ref, tasks = refs if side else (None, *refs)
    _, zp, zb, _, _, _ = place()
    width = labels_ref.shape[1]
    first = first_blocks()[side]
    lane = lax.broadcasted_iota(jnp.int32, (1, 2 * LAB_BLK), 1)
    upper = lane >= LAB_BLK
    offset = lane % LAB_BLK

    number = jnp.int32(0)
    for run in range(RUNS):
        column = (run // 4) * 128 + (zp * 2 + zb) * 4 + run % 4
        live = [live_ref[side * 4 + i, column] for i in range(4)]
        count = live[0] + live[1] + live[2] + live[3]
        low = jnp.where(live[0] > 0, 0, jnp.where(live[1] > 0, 1, jnp.where(live[2] > 0, 2, 3)))
        high = jnp.where(live[3] > 0, 3, jnp.where(live[2] > 0, 2, jnp.where(live[1] > 0, 1, 0)))
        tasks[4 * number] = run
        tasks[4 * number + 1] = low
        tasks[4 * number + 2] = high
        tasks[4 * number + 3] = count
        number = number + jnp.where(count > 0, 1, 0)

        @pl.when(count == 0)
        def _():
            rows = pl.ds(run * RUN, RUN)
            if side:
                out_ref[rows, :] = before_ref[rows, :].astype(out_ref.dtype)
            else:
                out_ref[rows, :] = jnp.zeros((RUN, width), out_ref.dtype)

    def work(task):
        run, low, high, count = (tasks[4 * task + i] for i in range(4))
        rows = pl.ds(pl.multiple_of(run * RUN, RUN), RUN)
        panel = jnp.concatenate(
            [
                labels_ref[pl.ds(pl.multiple_of(b * LAB_BLK, LAB_BLK), LAB_BLK), :]
                for b in (low, high)
            ],
            axis=0,
        )
        scores = SCALE * lax.dot_general(
            docs_ref[rows, :width],
            panel,
            (((1,), (1,)), ((), ())),
            preferred_element_type=jnp.float32,
        )
        places = docs_ref[rows, width:].astype(jnp.float32)
        pos_ids = places[:, :POS] * LAB_BLK + places[:, POS : 2 * POS]
        ids = ((first + jnp.where(upper, high, low)) * LAB_BLK + offset).astype(jnp.float32)
        hit = pos_ids[:, 0:1] == ids
        for k in range(1, POS):
            hit = hit | (pos_ids[:, k : k + 1] == ids)
        coef = SCALE * (jax.nn.sigmoid(scores) - jnp.where(hit, 1.0, 0.0))
        coef = jnp.where(upper & (count < 2), 0.0, coef).astype(jnp.bfloat16)
        total = jnp.dot(coef, panel, preferred_element_type=jnp.float32)
        if side:
            total = total + before_ref[rows, :]
        return rows, total.astype(out_ref.dtype)

    @pl.loop(0, (number + 1) // 2)
    def _(pair):
        results = [work(2 * pair), work(jnp.minimum(2 * pair + 1, number - 1))]
        for rows, total in results:
            out_ref[rows, :] = total


def finish_kernel(pieces_ref, doc_ref, out_ref):
    summed = pieces_ref[0].astype(jnp.float32)
    for i in range(1, PLANE_SIZE):
        summed = summed + pieces_ref[i].astype(jnp.float32)
    own_unit, own_norm = unit_rows(doc_ref[...])
    radial = jnp.sum(summed * own_unit, axis=-1, keepdims=True)
    out_ref[...] = (summed - radial * own_unit) / own_norm


def vmem(count):
    return [pl.BlockSpec(memory_space=pltpu.VMEM)] * count


def body(doc_emb, label_emb, short_blocks, short_len, positives):
    rows, width = doc_emb.shape
    label_half, spread = pl.pallas_call(
        prepare_kernel,
        out_shape=(
            jax.ShapeDtypeStruct(label_emb.shape, jnp.bfloat16),
            jax.ShapeDtypeStruct((PLANE_SIZE, rows, width + 128), jnp.bfloat16),
        ),
        in_specs=vmem(3),
        out_specs=(vmem(1)[0], pl.BlockSpec(memory_space=pl.ANY)),
        scratch_shapes=[
            pltpu.VMEM((rows, width + 128), jnp.bfloat16),
            pltpu.SemaphoreType.DMA((PLANE_SIZE,)),
        ],
    )(doc_emb, label_emb, positives.T)

    docs = lax.all_to_all(spread, PLANE, split_axis=0, concat_axis=0, tiled=True)
    docs = docs.reshape(PLANE_SIZE * rows, width + 128)
    pair = lax.all_gather(label_half, "zb", axis=0, tiled=True)
    own_labels = lax.all_gather(pair, "zp", axis=0, tiled=True)
    other_labels = lax.ppermute(own_labels, "c", [(0, 1), (1, 0)])

    grid = jnp.arange(4, dtype=jnp.int32)
    block_ids = jnp.concatenate([first + grid for first in first_blocks()])
    slot = jnp.arange(short_blocks.shape[1], dtype=jnp.int32)
    live = jnp.any(
        (short_blocks.T[None] == block_ids[:, None, None])
        & (slot[:, None] < short_len[None, :])[None],
        axis=1,
    ).astype(jnp.int32)

    def push(side, dtype, *operands):
        return pl.pallas_call(
            functools.partial(push_kernel, side),
            out_shape=jax.ShapeDtypeStruct((RUNS * RUN, width), dtype),
            in_specs=[pl.BlockSpec(memory_space=pltpu.SMEM)] + vmem(len(operands)),
            out_specs=vmem(1)[0],
            scratch_shapes=[pltpu.SMEM((4 * RUNS + 4,), jnp.int32)],
            compiler_params=pltpu.CompilerParams(vmem_limit_bytes=32 * 2**20),
            cost_estimate=pl.CostEstimate(
                flops=4 * RUNS * RUN * 2 * LAB_BLK * width,
                bytes_accessed=6 * 2**20,
                transcendentals=2 * RUNS * RUN * 2 * LAB_BLK,
            ),
        )(live, *operands)

    part = push(0, jnp.float32, docs, own_labels)
    part = push(1, jnp.bfloat16, docs, other_labels, part)
    pieces = lax.all_to_all(
        part.reshape(PLANE_SIZE, rows, width), PLANE, split_axis=0, concat_axis=0, tiled=True
    )
    return pl.pallas_call(
        finish_kernel,
        out_shape=jax.ShapeDtypeStruct((rows, width), jnp.float32),
        in_specs=vmem(2),
        out_specs=vmem(1)[0],
        compiler_params=pltpu.CompilerParams(vmem_limit_bytes=32 * 2**20),
    )(pieces, doc_emb)


def solution(mesh):
    fine = Mesh(mesh.devices.reshape(SIZES), AXES)
    doc, label = AXES[:3], AXES[3:]
    placed = (P(doc + label, None), P(label + doc, None), P(), P(), P(doc, None))
    return jax.shard_map(
        body, mesh=fine, in_specs=placed, out_specs=P(doc + label, None), check_vma=False
    )
```

```python
import functools

import jax
import jax.numpy as jnp
from jax import lax
from jax.experimental import pallas as pl
from jax.experimental.pallas import tpu as pltpu
from jax.sharding import Mesh, PartitionSpec as P

LAB_BLK = 128
POS = 8
SCALE = 16.0
RUN = 128
RUNS = 8

AXES = ("yh", "zp", "zb", "x", "yl", "c")
SIZES = (2, 16, 2, 4, 2, 2)
PLANE = ("yh", "x", "yl")
PLANE_SIZE = 16


def unit_rows(matrix):
    widened = matrix.astype(jnp.float32)
    row_norm = jnp.sqrt(jnp.sum(widened * widened, axis=-1, keepdims=True) + 1e-06)
    return widened / row_norm, row_norm


def place():
    return tuple(lax.axis_index(a) for a in AXES)


def first_blocks():
    yh, _, _, x, yl, core = place()
    shard = (x * 2 + yl) * 2 + core
    return shard * 8 + yh * 4, (shard + 1 - 2 * core) * 8 + yh * 4


def prepare_kernel(doc_ref, pos_ref, spread_ref, packed, sems):
    rows, width = doc_ref.shape
    packed[:, :width] = unit_rows(doc_ref[...])[0].astype(jnp.bfloat16)
    _, _, _, x, yl, core = place()
    ids = pos_ref[:, pl.ds(pl.multiple_of((x * 2 + yl) * 128, 128), 128)]
    parts = jnp.concatenate(
        [
            (ids // LAB_BLK).astype(jnp.float32),
            (ids % LAB_BLK).astype(jnp.float32),
            jnp.zeros((128 - 2 * POS, 128), jnp.float32),
        ],
        axis=0,
    )
    parts = parts.T
    packed[:, width:] = jnp.where(core == 0, parts[:rows], parts[rows:]).astype(jnp.bfloat16)
    copies = [
        pltpu.make_async_copy(packed, spread_ref.at[i], sems.at[i]) for i in range(PLANE_SIZE)
    ]
    for copy in copies:
        copy.start()
    for copy in copies:
        copy.wait()


def push_kernel(side, live_ref, docs_ref, labels_ref, *refs):
    before_ref, out_ref, tasks, select = refs if side else (None, *refs)
    _, zp, zb, _, _, _ = place()
    width = labels_ref.shape[1]
    first = first_blocks()[side]
    lane = lax.broadcasted_iota(jnp.int32, (1, LAB_BLK), 1)

    row = lax.broadcasted_iota(jnp.int32, select.shape, 0)
    group = lax.broadcasted_iota(jnp.int32, select.shape, 1) // 128
    select[...] = jnp.where(
        row == group, float(LAB_BLK), jnp.where(row == group + POS, 1.0, 0.0)
    ).astype(jnp.bfloat16)

    number = jnp.int32(0)
    for run in range(RUNS):
        column = (run // 4) * 128 + (zp * 2 + zb) * 4 + run % 4
        live = [live_ref[side * 4 + i, column] for i in range(4)]
        count = live[0] + live[1] + live[2] + live[3]
        low = jnp.where(live[0] > 0, 0, jnp.where(live[1] > 0, 1, jnp.where(live[2] > 0, 2, 3)))
        high = jnp.where(live[3] > 0, 3, jnp.where(live[2] > 0, 2, jnp.where(live[1] > 0, 1, 0)))
        tasks[4 * number] = run
        tasks[4 * number + 1] = low
        tasks[4 * number + 2] = high
        tasks[4 * number + 3] = count
        number = number + jnp.where(count > 0, 1, 0)

        @pl.when(count == 0)
        def _():
            rows = pl.ds(run * RUN, RUN)
            if side:
                out_ref[rows, :] = before_ref[rows, :].astype(out_ref.dtype)
            else:
                out_ref[rows, :] = jnp.zeros((RUN, width), out_ref.dtype)

    def coefficients(task):
        run, low, high, count = (tasks[4 * task + i] for i in range(4))
        rows = pl.ds(pl.multiple_of(run * RUN, RUN), RUN)
        panel = jnp.concatenate(
            [
                labels_ref[pl.ds(pl.multiple_of(b * LAB_BLK, LAB_BLK), LAB_BLK), :]
                for b in (low, high)
            ],
            axis=0,
        )
        scores = SCALE * lax.dot_general(
            docs_ref[rows, :width],
            panel,
            (((1,), (1,)), ((), ())),
            preferred_element_type=jnp.float32,
        )
        pos_ids = jnp.dot(docs_ref[rows, width:], select[...], preferred_element_type=jnp.float32)
        halves = []
        for i, block in enumerate((low, high)):
            ids = ((first + block) * LAB_BLK + lane).astype(jnp.float32)
            hit = pos_ids[:, :128] == ids
            for k in range(1, POS):
                hit = hit | (pos_ids[:, k * 128 : (k + 1) * 128] == ids)
            sigmoid = jax.nn.sigmoid(scores[:, i * LAB_BLK : (i + 1) * LAB_BLK])
            coef = SCALE * (sigmoid - jnp.where(hit, 1.0, 0.0))
            if i:
                coef = jnp.where(count > 1, coef, 0.0)
            halves.append(coef.astype(jnp.bfloat16))
        return rows, jnp.concatenate(halves, axis=1), panel

    @pl.loop(0, (number + 3) // 4)
    def _(batch):
        ready = [coefficients(jnp.minimum(4 * batch + i, number - 1)) for i in range(4)]
        for rows, coef, panel in ready:
            for start in range(0, width, 256):
                columns = slice(start, start + 256)
                total = jnp.dot(coef, panel[:, columns], preferred_element_type=jnp.float32)
                if side:
                    total = total + before_ref[rows, columns]
                out_ref[rows, columns] = total.astype(out_ref.dtype)


def finish_kernel(pieces_ref, doc_ref, out_ref):
    summed = pieces_ref[0].astype(jnp.float32)
    for i in range(1, PLANE_SIZE):
        summed = summed + pieces_ref[i].astype(jnp.float32)
    own_unit, own_norm = unit_rows(doc_ref[...])
    radial = jnp.sum(summed * own_unit, axis=-1, keepdims=True)
    out_ref[...] = (summed - radial * own_unit) / own_norm


def vmem(count):
    return [pl.BlockSpec(memory_space=pltpu.VMEM)] * count


def body(doc_emb, label_emb, short_blocks, short_len, positives):
    rows, width = doc_emb.shape
    neighbour = lax.ppermute(label_emb, "zb", [(0, 1), (1, 0)])
    spread = pl.pallas_call(
        prepare_kernel,
        out_shape=jax.ShapeDtypeStruct((PLANE_SIZE, rows, width + 128), jnp.bfloat16),
        in_specs=vmem(2),
        out_specs=pl.BlockSpec(memory_space=pl.ANY),
        scratch_shapes=[
            pltpu.VMEM((rows, width + 128), jnp.bfloat16),
            pltpu.SemaphoreType.DMA((PLANE_SIZE,)),
        ],
        cost_estimate=pl.CostEstimate(
            flops=8 * rows * width, bytes_accessed=8 * 2**20, transcendentals=rows
        ),
    )(doc_emb, positives.T)
    docs = lax.all_to_all(spread, PLANE, split_axis=0, concat_axis=0, tiled=True)
    docs = docs.reshape(PLANE_SIZE * rows, width + 128)
    even = lax.axis_index("zb") == 0
    pair = jnp.stack(
        [jnp.where(even, label_emb, neighbour), jnp.where(even, neighbour, label_emb)]
    ).reshape(2 * label_emb.shape[0], width)
    pair = unit_rows(pair)[0].astype(jnp.bfloat16)
    own_labels = lax.all_gather(pair, "zp", axis=0, tiled=True)
    other_labels = lax.ppermute(own_labels, "c", [(0, 1), (1, 0)])

    grid = jnp.arange(4, dtype=jnp.int32)
    block_ids = jnp.concatenate([first + grid for first in first_blocks()])
    slot = jnp.arange(short_blocks.shape[1], dtype=jnp.int32)
    live = jnp.any(
        (short_blocks.T[None] == block_ids[:, None, None])
        & (slot[:, None] < short_len[None, :])[None],
        axis=1,
    ).astype(jnp.int32)

    def push(side, dtype, *operands):
        return pl.pallas_call(
            functools.partial(push_kernel, side),
            out_shape=jax.ShapeDtypeStruct((RUNS * RUN, width), dtype),
            in_specs=[pl.BlockSpec(memory_space=pltpu.SMEM)] + vmem(len(operands)),
            out_specs=vmem(1)[0],
            scratch_shapes=[
                pltpu.SMEM((4 * RUNS + 4,), jnp.int32),
                pltpu.VMEM((128, POS * 128), jnp.bfloat16),
            ],
            compiler_params=pltpu.CompilerParams(vmem_limit_bytes=32 * 2**20),
            cost_estimate=pl.CostEstimate(
                flops=4 * RUNS * RUN * 2 * LAB_BLK * width,
                bytes_accessed=6 * 2**20,
                transcendentals=2 * RUNS * RUN * 2 * LAB_BLK,
            ),
        )(live, *operands)

    part = push(0, jnp.float32, docs, own_labels)
    part = push(1, jnp.bfloat16, docs, other_labels, part)
    pieces = lax.all_to_all(
        part.reshape(PLANE_SIZE, rows, width), PLANE, split_axis=0, concat_axis=0, tiled=True
    )
    return pl.pallas_call(
        finish_kernel,
        out_shape=jax.ShapeDtypeStruct((rows, width), jnp.float32),
        in_specs=vmem(2),
        out_specs=vmem(1)[0],
        compiler_params=pltpu.CompilerParams(vmem_limit_bytes=32 * 2**20),
    )(pieces, doc_emb)


def solution(mesh):
    fine = Mesh(mesh.devices.reshape(SIZES), AXES)
    doc, label = AXES[:3], AXES[3:]
    placed = (P(doc + label, None), P(label + doc, None), P(), P(), P(doc, None))
    return jax.shard_map(
        body, mesh=fine, in_specs=placed, out_specs=P(doc + label, None), check_vma=False
    )
```

```python
import jax
import jax.numpy as jnp
from jax import lax
from jax.experimental import pallas as pl
from jax.experimental.pallas import tpu as pltpu
from jax.sharding import Mesh, PartitionSpec as P

LAB_BLK = 128
POS = 8
SCALE = 16.0
RUN = 128
RUNS = 8

AXES = ("yh", "zp", "zb", "x", "yl", "c")
SIZES = (2, 16, 2, 4, 2, 2)
PLANE = ("yh", "x", "yl")
PLANE_SIZE = 16


def unit_rows(matrix):
    widened = matrix.astype(jnp.float32)
    row_norm = jnp.sqrt(jnp.sum(widened * widened, axis=-1, keepdims=True) + 1e-06)
    return widened / row_norm, row_norm


def place():
    return tuple(lax.axis_index(a) for a in AXES)


def first_block(side):
    yh, _, _, x, yl, _ = place()
    return ((x * 2 + yl) * 2 + side) * 8 + yh * 4


def prepare_kernel(doc_ref, other_ref, pos_ref, spread_ref, packed, sems):
    rows, width = doc_ref.shape
    packed[:rows, :width] = unit_rows(doc_ref[...])[0].astype(jnp.bfloat16)
    packed[rows:, :width] = unit_rows(other_ref[...])[0].astype(jnp.bfloat16)
    _, _, _, x, yl, _ = place()
    ids = pos_ref[:, pl.ds(pl.multiple_of((x * 2 + yl) * 128, 128), 128)]
    parts = jnp.concatenate(
        [
            (ids // LAB_BLK).astype(jnp.float32),
            (ids % LAB_BLK).astype(jnp.float32),
            jnp.zeros((128 - 2 * POS, 128), jnp.float32),
        ],
        axis=0,
    )
    packed[:, width:] = parts.T.astype(jnp.bfloat16)
    copies = [
        pltpu.make_async_copy(packed, spread_ref.at[i], sems.at[i]) for i in range(PLANE_SIZE)
    ]
    for copy in copies:
        copy.start()
    for copy in copies:
        copy.wait()


def push_kernel(live_ref, kept_ref, sent_ref, got_ref, out_ref, tasks, select, total):
    core = place()[-1]
    for mine, docs_ref, labels_ref in ((0, kept_ref, got_ref), (1, got_ref, sent_ref)):

        @pl.when(core == mine)
        def _():
            push_side(0, live_ref, docs_ref, labels_ref, None, total, tasks, select)
            push_side(1, live_ref, docs_ref, labels_ref, total, out_ref, tasks, select)


def push_side(side, live_ref, docs_ref, labels_ref, before_ref, out_ref, tasks, select):
    _, zp, zb, _, _, _ = place()
    width = out_ref.shape[1]
    first = first_block(side)
    lane = lax.broadcasted_iota(jnp.int32, (1, LAB_BLK), 1)

    row = lax.broadcasted_iota(jnp.int32, select.shape, 0)
    group = lax.broadcasted_iota(jnp.int32, select.shape, 1) // 128
    select[...] = jnp.where(
        row == group, float(LAB_BLK), jnp.where(row == group + POS, 1.0, 0.0)
    ).astype(jnp.bfloat16)

    number = jnp.int32(0)
    for run in range(RUNS):
        column = (run // 4) * 128 + (zp * 2 + zb) * 4 + run % 4
        live = [live_ref[side * 4 + i, column] for i in range(4)]
        count = live[0] + live[1] + live[2] + live[3]
        low = jnp.where(live[0] > 0, 0, jnp.where(live[1] > 0, 1, jnp.where(live[2] > 0, 2, 3)))
        high = jnp.where(live[3] > 0, 3, jnp.where(live[2] > 0, 2, jnp.where(live[1] > 0, 1, 0)))
        tasks[4 * number] = run
        tasks[4 * number + 1] = low
        tasks[4 * number + 2] = high
        tasks[4 * number + 3] = count
        number = number + jnp.where(count > 0, 1, 0)

        @pl.when(count == 0)
        def _():
            rows = pl.ds(run * RUN, RUN)
            if side:
                out_ref[rows, :] = before_ref[rows, :].astype(out_ref.dtype)
            else:
                out_ref[rows, :] = jnp.zeros((RUN, width), out_ref.dtype)

    def coefficients(task):
        run, low, high, count = (tasks[4 * task + i] for i in range(4))
        rows = pl.ds(pl.multiple_of(run * RUN, RUN), RUN)
        panel = jnp.concatenate(
            [
                labels_ref[pl.ds(pl.multiple_of((4 * side + b) * LAB_BLK, LAB_BLK), LAB_BLK), :width]
                for b in (low, high)
            ],
            axis=0,
        )
        scores = SCALE * lax.dot_general(
            docs_ref[rows, :width],
            panel,
            (((1,), (1,)), ((), ())),
            preferred_element_type=jnp.float32,
        )
        pos_ids = jnp.dot(docs_ref[rows, width:], select[...], preferred_element_type=jnp.float32)
        halves = []
        for i, block in enumerate((low, high)):
            ids = ((first + block) * LAB_BLK + lane).astype(jnp.float32)
            hit = pos_ids[:, :128] == ids
            for k in range(1, POS):
                hit = hit | (pos_ids[:, k * 128 : (k + 1) * 128] == ids)
            sigmoid = jax.nn.sigmoid(scores[:, i * LAB_BLK : (i + 1) * LAB_BLK])
            coef = SCALE * (sigmoid - jnp.where(hit, 1.0, 0.0))
            if i:
                coef = jnp.where(count > 1, coef, 0.0)
            halves.append(coef.astype(jnp.bfloat16))
        return rows, jnp.concatenate(halves, axis=1), panel

    @pl.loop(0, (number + 3) // 4)
    def _(batch):
        ready = [coefficients(jnp.minimum(4 * batch + i, number - 1)) for i in range(4)]
        for rows, coef, panel in ready:
            for start in range(0, width, 256):
                columns = slice(start, start + 256)
                total = jnp.dot(coef, panel[:, columns], preferred_element_type=jnp.float32)
                if side:
                    total = total + before_ref[rows, columns]
                out_ref[rows, columns] = total.astype(out_ref.dtype)


def finish_kernel(pieces_ref, doc_ref, out_ref):
    summed = pieces_ref[0].astype(jnp.float32)
    for i in range(1, PLANE_SIZE):
        summed = summed + pieces_ref[i].astype(jnp.float32)
    own_unit, own_norm = unit_rows(doc_ref[...])
    radial = jnp.sum(summed * own_unit, axis=-1, keepdims=True)
    out_ref[...] = (summed - radial * own_unit) / own_norm


def vmem(count):
    return [pl.BlockSpec(memory_space=pltpu.VMEM)] * count


def body(doc_emb, label_emb, short_blocks, short_len, positives):
    rows, width = doc_emb.shape
    other_docs = lax.ppermute(doc_emb, "c", [(0, 1), (1, 0)])
    near_labels = lax.all_gather(label_emb, ("zb", "c"), axis=0, tiled=True)

    def gather_labels(operands):
        half = unit_rows(operands[2])[0].astype(jnp.bfloat16)
        labels = lax.all_gather(half.astype(jnp.float16), "zp", axis=0, tiled=True)
        labels = labels.reshape(16, 2, 2, label_emb.shape[0], width).transpose(2, 0, 1, 3, 4)
        labels = labels.reshape(-1, width).astype(jnp.bfloat16)
        labels = jnp.pad(labels, ((0, 0), (0, 128)))
        return jnp.zeros_like(labels), labels

    def gather_docs(operands):
        spread = pl.pallas_call(
            prepare_kernel,
            out_shape=jax.ShapeDtypeStruct((PLANE_SIZE, 2 * rows, width + 128), jnp.bfloat16),
            in_specs=vmem(3),
            out_specs=pl.BlockSpec(memory_space=pl.ANY),
            scratch_shapes=[
                pltpu.VMEM((2 * rows, width + 128), jnp.bfloat16),
                pltpu.SemaphoreType.DMA((PLANE_SIZE,)),
            ],
        )(operands[0], operands[1], operands[3])
        docs = lax.all_to_all(spread, PLANE, split_axis=0, concat_axis=0, tiled=True)
        return tuple(docs[:, i * rows : (i + 1) * rows].reshape(-1, width + 128) for i in range(2))

    kept, sent = lax.cond(
        lax.axis_index("c") == 1,
        gather_labels,
        gather_docs,
        (doc_emb, other_docs, near_labels, positives.T),
    )
    got = lax.ppermute(sent, "c", [(0, 1), (1, 0)])

    grid = jnp.arange(4, dtype=jnp.int32)
    block_ids = jnp.concatenate([first_block(side) + grid for side in range(2)])
    slot = jnp.arange(short_blocks.shape[1], dtype=jnp.int32)
    live = jnp.any(
        (short_blocks.T[None] == block_ids[:, None, None])
        & (slot[:, None] < short_len[None, :])[None],
        axis=1,
    ).astype(jnp.int32)

    part = pl.pallas_call(
        push_kernel,
        out_shape=jax.ShapeDtypeStruct((RUNS * RUN, width), jnp.bfloat16),
        in_specs=[pl.BlockSpec(memory_space=pltpu.SMEM)] + vmem(3),
        out_specs=vmem(1)[0],
        scratch_shapes=[
            pltpu.SMEM((4 * RUNS + 4,), jnp.int32),
            pltpu.VMEM((128, POS * 128), jnp.bfloat16),
            pltpu.VMEM((RUNS * RUN, width), jnp.float32),
        ],
        compiler_params=pltpu.CompilerParams(vmem_limit_bytes=32 * 2**20),
    )(live, kept, sent, got)
    pieces = lax.all_to_all(
        part.reshape(PLANE_SIZE, rows, width), PLANE, split_axis=0, concat_axis=0, tiled=True
    )
    return pl.pallas_call(
        finish_kernel,
        out_shape=jax.ShapeDtypeStruct((rows, width), jnp.float32),
        in_specs=vmem(2),
        out_specs=vmem(1)[0],
        compiler_params=pltpu.CompilerParams(vmem_limit_bytes=32 * 2**20),
    )(pieces, doc_emb)


def solution(mesh):
    fine = Mesh(mesh.devices.reshape(SIZES), AXES)
    doc, label = AXES[:3], AXES[3:]
    placed = (P(doc + label, None), P(label + doc, None), P(), P(), P(doc, None))
    return jax.shard_map(
        body, mesh=fine, in_specs=placed, out_specs=P(doc + label, None), check_vma=False
    )
```

```python
import functools

import jax
import jax.numpy as jnp
from jax import lax
from jax.experimental import pallas as pl
from jax.experimental.pallas import tpu as pltpu
from jax.sharding import Mesh, PartitionSpec as P

LAB_BLK = 128
POS = 8
SCALE = 16.0
RUN = 128
RUNS = 8

AXES = ("yh", "zp", "zb", "x", "yl", "c")
SIZES = (2, 16, 2, 4, 2, 2)
PLANE = ("yh", "x", "yl")
PLANE_SIZE = 16


def unit_rows(matrix):
    widened = matrix.astype(jnp.float32)
    row_norm = jnp.sqrt(jnp.sum(widened * widened, axis=-1, keepdims=True) + 1e-06)
    return widened / row_norm, row_norm


def place():
    return tuple(lax.axis_index(a) for a in AXES)


def first_blocks():
    yh, _, _, x, yl, core = place()
    shard = (x * 2 + yl) * 2 + core
    return shard * 8 + yh * 4, (shard + 1 - 2 * core) * 8 + yh * 4


def prepare_kernel(doc_ref, pos_ref, spread_ref, packed, sems):
    rows, width = doc_ref.shape
    packed[:, :width] = unit_rows(doc_ref[...])[0].astype(jnp.bfloat16)
    _, _, _, x, yl, core = place()
    ids = pos_ref[:, pl.ds(pl.multiple_of((x * 2 + yl) * 128, 128), 128)]
    parts = jnp.concatenate(
        [
            (ids // LAB_BLK).astype(jnp.float32),
            (ids % LAB_BLK).astype(jnp.float32),
            jnp.zeros((128 - 2 * POS, 128), jnp.float32),
        ],
        axis=0,
    )
    parts = parts.T
    packed[:, width:] = jnp.where(core == 0, parts[:rows], parts[rows:]).astype(jnp.bfloat16)
    copies = [
        pltpu.make_async_copy(packed, spread_ref.at[i], sems.at[i]) for i in range(PLANE_SIZE)
    ]
    for copy in copies:
        copy.start()
    for copy in copies:
        copy.wait()


def push_kernel(side, live_ref, docs_ref, labels_ref, *refs):
    before_ref, out_ref, tasks, select = refs if side else (None, *refs)
    _, zp, zb, _, _, _ = place()
    width = labels_ref.shape[1]
    first = first_blocks()[side]
    lane = lax.broadcasted_iota(jnp.int32, (1, LAB_BLK), 1)

    row = lax.broadcasted_iota(jnp.int32, select.shape, 0)
    group = lax.broadcasted_iota(jnp.int32, select.shape, 1) // 128
    select[...] = jnp.where(
        row == group, float(LAB_BLK), jnp.where(row == group + POS, 1.0, 0.0)
    ).astype(jnp.bfloat16)

    def listed(which, run):
        column = (run // 4) * 128 + (zp * 2 + zb) * 4 + run % 4
        live = [live_ref[which * 4 + i, column] for i in range(4)]
        low = jnp.where(live[0] > 0, 0, jnp.where(live[1] > 0, 1, jnp.where(live[2] > 0, 2, 3)))
        high = jnp.where(live[3] > 0, 3, jnp.where(live[2] > 0, 2, jnp.where(live[1] > 0, 1, 0)))
        return live[0] + live[1] + live[2] + live[3], low, high

    number = jnp.int32(0)
    for run in range(RUNS):
        count, low, high = listed(side, run)
        begun = listed(0, run)[0] if side else jnp.int32(0)
        for i, value in enumerate((run, low, high, count, begun)):
            tasks[5 * number + i] = value
        number = number + jnp.where(count > 0, 1, 0)
        if side:
            rows = pl.ds(run * RUN, RUN)

            @pl.when((count == 0) & (begun > 0))
            def _():
                out_ref[rows, :] = before_ref[rows, :].astype(out_ref.dtype)

            @pl.when((count == 0) & (begun == 0))
            def _():
                out_ref[rows, :] = jnp.zeros((RUN, width), out_ref.dtype)

    def coefficients(task):
        run, low, high, count, begun = (tasks[5 * task + i] for i in range(5))
        rows = pl.ds(pl.multiple_of(run * RUN, RUN), RUN)
        panel = jnp.concatenate(
            [
                labels_ref[pl.ds(pl.multiple_of(b * LAB_BLK, LAB_BLK), LAB_BLK), :]
                for b in (low, high)
            ],
            axis=0,
        )
        scores = SCALE * lax.dot_general(
            docs_ref[rows, :width],
            panel,
            (((1,), (1,)), ((), ())),
            preferred_element_type=jnp.float32,
        )
        pos_ids = jnp.dot(docs_ref[rows, width:], select[...], preferred_element_type=jnp.float32)
        halves = []
        for i, block in enumerate((low, high)):
            ids = ((first + block) * LAB_BLK + lane).astype(jnp.float32)
            hit = pos_ids[:, :128] == ids
            for k in range(1, POS):
                hit = hit | (pos_ids[:, k * 128 : (k + 1) * 128] == ids)
            sigmoid = jax.nn.sigmoid(scores[:, i * LAB_BLK : (i + 1) * LAB_BLK])
            coef = SCALE * (sigmoid - jnp.where(hit, 1.0, 0.0))
            if i:
                coef = jnp.where(count > 1, coef, 0.0)
            halves.append(coef.astype(jnp.bfloat16))
        return rows, jnp.concatenate(halves, axis=1), panel, begun

    def batch(start, size):
        ready = [coefficients(jnp.minimum(start + i, number - 1)) for i in range(size)]
        for rows, coef, panel, begun in ready:
            for left in range(0, width, 256):
                columns = slice(left, left + 256)
                total = jnp.dot(coef, panel[:, columns], preferred_element_type=jnp.float32)
                if side:
                    total = jnp.where(begun > 0, total + before_ref[rows, columns], total)
                out_ref[rows, columns] = total.astype(out_ref.dtype)

    rest = number % 4

    @pl.loop(0, (number + 1) // 4)
    def _(i):
        batch(4 * i, 4)

    @pl.when((rest == 1) | (rest == 2))
    def _():
        batch(number - rest, 2)


def finish_kernel(pieces_ref, doc_ref, out_ref):
    summed = pieces_ref[0].astype(jnp.float32)
    for i in range(1, PLANE_SIZE):
        summed = summed + pieces_ref[i].astype(jnp.float32)
    own_unit, own_norm = unit_rows(doc_ref[...])
    radial = jnp.sum(summed * own_unit, axis=-1, keepdims=True)
    out_ref[...] = (summed - radial * own_unit) / own_norm


def vmem(count):
    return [pl.BlockSpec(memory_space=pltpu.VMEM)] * count


def body(doc_emb, label_emb, short_blocks, short_len, positives):
    rows, width = doc_emb.shape
    neighbour = lax.ppermute(label_emb, "zb", [(0, 1), (1, 0)])
    spread = pl.pallas_call(
        prepare_kernel,
        out_shape=jax.ShapeDtypeStruct((PLANE_SIZE, rows, width + 128), jnp.bfloat16),
        in_specs=vmem(2),
        out_specs=pl.BlockSpec(memory_space=pl.ANY),
        scratch_shapes=[
            pltpu.VMEM((rows, width + 128), jnp.bfloat16),
            pltpu.SemaphoreType.DMA((PLANE_SIZE,)),
        ],
        cost_estimate=pl.CostEstimate(
            flops=8 * rows * width, bytes_accessed=8 * 2**20, transcendentals=rows
        ),
    )(doc_emb, positives.T)
    docs = lax.all_to_all(spread, PLANE, split_axis=0, concat_axis=0, tiled=True)
    docs = docs.reshape(PLANE_SIZE * rows, width + 128)
    even = lax.axis_index("zb") == 0
    pair = jnp.stack(
        [jnp.where(even, label_emb, neighbour), jnp.where(even, neighbour, label_emb)]
    ).reshape(2 * label_emb.shape[0], width)
    pair = unit_rows(pair)[0].astype(jnp.bfloat16)
    own_labels = lax.all_gather(pair, "zp", axis=0, tiled=True)
    other_labels = lax.ppermute(own_labels, "c", [(0, 1), (1, 0)])

    grid = jnp.arange(4, dtype=jnp.int32)
    block_ids = jnp.concatenate([first + grid for first in first_blocks()])
    slot = jnp.arange(short_blocks.shape[1], dtype=jnp.int32)
    live = jnp.any(
        (short_blocks.T[None] == block_ids[:, None, None])
        & (slot[:, None] < short_len[None, :])[None],
        axis=1,
    ).astype(jnp.int32)

    def push(side, dtype, *operands):
        return pl.pallas_call(
            functools.partial(push_kernel, side),
            out_shape=jax.ShapeDtypeStruct((RUNS * RUN, width), dtype),
            in_specs=[pl.BlockSpec(memory_space=pltpu.SMEM)] + vmem(len(operands)),
            out_specs=vmem(1)[0],
            scratch_shapes=[
                pltpu.SMEM((5 * RUNS,), jnp.int32),
                pltpu.VMEM((128, POS * 128), jnp.bfloat16),
            ],
            compiler_params=pltpu.CompilerParams(vmem_limit_bytes=32 * 2**20),
            cost_estimate=pl.CostEstimate(
                flops=4 * RUNS * RUN * 2 * LAB_BLK * width,
                bytes_accessed=6 * 2**20,
                transcendentals=2 * RUNS * RUN * 2 * LAB_BLK,
            ),
        )(live, *operands)

    part = push(0, jnp.float32, docs, own_labels)
    part = push(1, jnp.bfloat16, docs, other_labels, part)
    pieces = lax.all_to_all(
        part.reshape(PLANE_SIZE, rows, width), PLANE, split_axis=0, concat_axis=0, tiled=True
    )
    return pl.pallas_call(
        finish_kernel,
        out_shape=jax.ShapeDtypeStruct((rows, width), jnp.float32),
        in_specs=vmem(2),
        out_specs=vmem(1)[0],
        compiler_params=pltpu.CompilerParams(vmem_limit_bytes=32 * 2**20),
    )(pieces, doc_emb)


def solution(mesh):
    fine = Mesh(mesh.devices.reshape(SIZES), AXES)
    doc, label = AXES[:3], AXES[3:]
    placed = (P(doc + label, None), P(label + doc, None), P(), P(), P(doc, None))
    return jax.shard_map(
        body, mesh=fine, in_specs=placed, out_specs=P(doc + label, None), check_vma=False
    )
```

```python
import functools

import jax
import jax.numpy as jnp
from jax import lax
from jax.experimental import pallas as pl
from jax.experimental.pallas import tpu as pltpu
from jax.sharding import Mesh, PartitionSpec as P

LAB_BLK = 128
POS = 8
SCALE = 16.0
RUN = 128
RUNS = 8

AXES = ("yh", "zp", "zb", "x", "yl", "c")
SIZES = (2, 16, 2, 4, 2, 2)
PLANE = ("yh", "x", "yl")
PLANE_SIZE = 16


def unit_rows(matrix):
    widened = matrix.astype(jnp.float32)
    row_norm = jnp.sqrt(jnp.sum(widened * widened, axis=-1, keepdims=True) + 1e-06)
    return widened / row_norm, row_norm


def place():
    return tuple(lax.axis_index(a) for a in AXES)


def first_blocks():
    yh, _, _, x, yl, core = place()
    shard = (x * 2 + yl) * 2 + core
    return shard * 8 + yh * 4, (shard + 1 - 2 * core) * 8 + yh * 4


def prepare_kernel(doc_ref, pos_ref, blocks_ref, len_ref, spread_ref, live_ref, packed, sems):
    rows, width = doc_ref.shape
    packed[:, :width] = unit_rows(doc_ref[...])[0].astype(jnp.bfloat16)
    _, _, _, x, yl, core = place()
    ids = pos_ref[:, pl.ds(pl.multiple_of((x * 2 + yl) * 128, 128), 128)]
    parts = jnp.concatenate(
        [
            (ids // LAB_BLK).astype(jnp.float32),
            (ids % LAB_BLK).astype(jnp.float32),
            jnp.zeros((128 - 2 * POS, 128), jnp.float32),
        ],
        axis=0,
    )
    parts = parts.T
    packed[:, width:] = jnp.where(core == 0, parts[:rows], parts[rows:]).astype(jnp.bfloat16)
    copies = [
        pltpu.make_async_copy(packed, spread_ref.at[i], sems.at[i]) for i in range(PLANE_SIZE)
    ]
    for copy in copies:
        copy.start()
    listed = blocks_ref[...]
    slot = lax.broadcasted_iota(jnp.int32, listed.shape, 0)
    listed = jnp.where(slot < len_ref[...], listed, -1)
    for i in range(8):
        block = first_blocks()[i // 4] + i % 4
        hits = jnp.where(listed == block, 1, 0)
        live_ref[i : i + 1, :] = jnp.max(hits, axis=0, keepdims=True)
    for copy in copies:
        copy.wait()


def push_kernel(side, live_ref, docs_ref, labels_ref, *refs):
    before_ref, out_ref, tasks, select = refs if side else (None, *refs)
    _, zp, zb, _, _, _ = place()
    width = labels_ref.shape[1]
    first = first_blocks()[side]
    lane = lax.broadcasted_iota(jnp.int32, (1, LAB_BLK), 1)

    row = lax.broadcasted_iota(jnp.int32, select.shape, 0)
    group = lax.broadcasted_iota(jnp.int32, select.shape, 1) // 128
    select[...] = jnp.where(
        row == group, float(LAB_BLK), jnp.where(row == group + POS, 1.0, 0.0)
    ).astype(jnp.bfloat16)

    def listed(which, run):
        column = (run // 4) * 128 + (zp * 2 + zb) * 4 + run % 4
        live = [live_ref[which * 4 + i, column] for i in range(4)]
        low = jnp.where(live[0] > 0, 0, jnp.where(live[1] > 0, 1, jnp.where(live[2] > 0, 2, 3)))
        high = jnp.where(live[3] > 0, 3, jnp.where(live[2] > 0, 2, jnp.where(live[1] > 0, 1, 0)))
        return live[0] + live[1] + live[2] + live[3], low, high

    number = jnp.int32(0)
    for run in range(RUNS):
        count, low, high = listed(side, run)
        begun = listed(0, run)[0] if side else jnp.int32(0)
        for i, value in enumerate((run, low, high, count, begun)):
            tasks[5 * number + i] = value
        number = number + jnp.where(count > 0, 1, 0)
        if side:
            rows = pl.ds(run * RUN, RUN)

            @pl.when((count == 0) & (begun > 0))
            def _():
                out_ref[rows, :] = before_ref[rows, :].astype(out_ref.dtype)

            @pl.when((count == 0) & (begun == 0))
            def _():
                out_ref[rows, :] = jnp.zeros((RUN, width), out_ref.dtype)

    def coefficients(task):
        run, low, high, count, begun = (tasks[5 * task + i] for i in range(5))
        rows = pl.ds(pl.multiple_of(run * RUN, RUN), RUN)
        panel = jnp.concatenate(
            [
                labels_ref[pl.ds(pl.multiple_of(b * LAB_BLK, LAB_BLK), LAB_BLK), :]
                for b in (low, high)
            ],
            axis=0,
        )
        scores = SCALE * lax.dot_general(
            docs_ref[rows, :width],
            panel,
            (((1,), (1,)), ((), ())),
            preferred_element_type=jnp.float32,
        )
        pos_ids = jnp.dot(docs_ref[rows, width:], select[...], preferred_element_type=jnp.float32)
        halves = []
        for i, block in enumerate((low, high)):
            ids = ((first + block) * LAB_BLK + lane).astype(jnp.float32)
            hit = pos_ids[:, :128] == ids
            for k in range(1, POS):
                hit = hit | (pos_ids[:, k * 128 : (k + 1) * 128] == ids)
            sigmoid = jax.nn.sigmoid(scores[:, i * LAB_BLK : (i + 1) * LAB_BLK])
            coef = SCALE * (sigmoid - jnp.where(hit, 1.0, 0.0))
            if i:
                coef = jnp.where(count > 1, coef, 0.0)
            halves.append(coef.astype(jnp.bfloat16))
        return rows, jnp.concatenate(halves, axis=1), panel, begun

    def batch(start, size):
        ready = [coefficients(jnp.minimum(start + i, number - 1)) for i in range(size)]
        for rows, coef, panel, begun in ready:
            for left in range(0, width, 256):
                columns = slice(left, left + 256)
                total = jnp.dot(coef, panel[:, columns], preferred_element_type=jnp.float32)
                if side:
                    total = jnp.where(begun > 0, total + before_ref[rows, columns], total)
                out_ref[rows, columns] = total.astype(out_ref.dtype)

    rest = number % 4

    @pl.loop(0, (number + 1) // 4)
    def _(i):
        batch(4 * i, 4)

    @pl.when((rest == 1) | (rest == 2))
    def _():
        batch(number - rest, 2)


def finish_kernel(pieces_ref, doc_ref, out_ref):
    summed = pieces_ref[0].astype(jnp.float32)
    for i in range(1, PLANE_SIZE):
        summed = summed + pieces_ref[i].astype(jnp.float32)
    own_unit, own_norm = unit_rows(doc_ref[...])
    radial = jnp.sum(summed * own_unit, axis=-1, keepdims=True)
    out_ref[...] = (summed - radial * own_unit) / own_norm


def vmem(count):
    return [pl.BlockSpec(memory_space=pltpu.VMEM)] * count


def body(doc_emb, label_emb, short_blocks, short_len, positives):
    rows, width = doc_emb.shape
    neighbour = lax.ppermute(label_emb, "zb", [(0, 1), (1, 0)])
    spread, live = pl.pallas_call(
        prepare_kernel,
        out_shape=(
            jax.ShapeDtypeStruct((PLANE_SIZE, rows, width + 128), jnp.bfloat16),
            jax.ShapeDtypeStruct((8, short_blocks.shape[0]), jnp.int32),
        ),
        in_specs=vmem(4),
        out_specs=(pl.BlockSpec(memory_space=pl.ANY), vmem(1)[0]),
        scratch_shapes=[
            pltpu.VMEM((rows, width + 128), jnp.bfloat16),
            pltpu.SemaphoreType.DMA((PLANE_SIZE,)),
        ],
        cost_estimate=pl.CostEstimate(
            flops=8 * rows * width, bytes_accessed=8 * 2**20, transcendentals=rows
        ),
    )(doc_emb, positives.T, short_blocks.T, short_len.reshape(1, -1))
    docs = lax.all_to_all(spread, PLANE, split_axis=0, concat_axis=0, tiled=True)
    docs = docs.reshape(PLANE_SIZE * rows, width + 128)
    even = lax.axis_index("zb") == 0
    pair = jnp.stack(
        [jnp.where(even, label_emb, neighbour), jnp.where(even, neighbour, label_emb)]
    ).reshape(2 * label_emb.shape[0], width)
    pair = unit_rows(pair)[0].astype(jnp.bfloat16)
    own_labels = lax.all_gather(pair, "zp", axis=0, tiled=True)
    other_labels = lax.ppermute(own_labels, "c", [(0, 1), (1, 0)])

    def push(side, dtype, *operands):
        return pl.pallas_call(
            functools.partial(push_kernel, side),
            out_shape=jax.ShapeDtypeStruct((RUNS * RUN, width), dtype),
            in_specs=[pl.BlockSpec(memory_space=pltpu.SMEM)] + vmem(len(operands)),
            out_specs=vmem(1)[0],
            scratch_shapes=[
                pltpu.SMEM((5 * RUNS,), jnp.int32),
                pltpu.VMEM((128, POS * 128), jnp.bfloat16),
            ],
            compiler_params=pltpu.CompilerParams(vmem_limit_bytes=32 * 2**20),
            cost_estimate=pl.CostEstimate(
                flops=4 * RUNS * RUN * 2 * LAB_BLK * width,
                bytes_accessed=6 * 2**20,
                transcendentals=2 * RUNS * RUN * 2 * LAB_BLK,
            ),
        )(live, *operands)

    part = push(0, jnp.float32, docs, own_labels)
    part = push(1, jnp.bfloat16, docs, other_labels, part)
    pieces = lax.all_to_all(
        part.reshape(PLANE_SIZE, rows, width), PLANE, split_axis=0, concat_axis=0, tiled=True
    )
    return pl.pallas_call(
        finish_kernel,
        out_shape=jax.ShapeDtypeStruct((rows, width), jnp.float32),
        in_specs=vmem(2),
        out_specs=vmem(1)[0],
        compiler_params=pltpu.CompilerParams(vmem_limit_bytes=32 * 2**20),
    )(pieces, doc_emb)


def solution(mesh):
    fine = Mesh(mesh.devices.reshape(SIZES), AXES)
    doc, label = AXES[:3], AXES[3:]
    placed = (P(doc + label, None), P(label + doc, None), P(), P(), P(doc, None))
    return jax.shard_map(
        body, mesh=fine, in_specs=placed, out_specs=P(doc + label, None), check_vma=False
    )
```

```python
import functools

import jax
import jax.numpy as jnp
from jax import lax
from jax.experimental import pallas as pl
from jax.experimental.pallas import tpu as pltpu
from jax.sharding import Mesh, PartitionSpec as P

LAB_BLK = 128
POS = 8
SCALE = 16.0
RUN = 128
RUNS = 8

AXES = ("yh", "zp", "zb", "x", "yl", "c")
SIZES = (2, 16, 2, 4, 2, 2)
PLANE = ("yh", "x", "yl")
PLANE_SIZE = 16


def unit_rows(matrix):
    widened = matrix.astype(jnp.float32)
    row_norm = jnp.sqrt(jnp.sum(widened * widened, axis=-1, keepdims=True) + 1e-06)
    return widened / row_norm, row_norm


def place():
    return tuple(lax.axis_index(a) for a in AXES)


def first_blocks():
    yh, _, _, x, yl, core = place()
    shard = (x * 2 + yl) * 2 + core
    return shard * 8 + yh * 4, (shard + 1 - 2 * core) * 8 + yh * 4


def prepare_kernel(doc_ref, pos_ref, spread_ref, packed, sems):
    rows, width = doc_ref.shape
    packed[:, :width] = unit_rows(doc_ref[...])[0].astype(jnp.bfloat16)
    _, _, _, x, yl, core = place()
    ids = pos_ref[:, pl.ds(pl.multiple_of((x * 2 + yl) * 128, 128), 128)]
    parts = jnp.concatenate(
        [
            (ids // LAB_BLK).astype(jnp.float32),
            (ids % LAB_BLK).astype(jnp.float32),
            jnp.zeros((128 - 2 * POS, 128), jnp.float32),
        ],
        axis=0,
    )
    parts = parts.T
    packed[:, width:] = jnp.where(core == 0, parts[:rows], parts[rows:]).astype(jnp.bfloat16)
    copies = [
        pltpu.make_async_copy(packed, spread_ref.at[i], sems.at[i]) for i in range(PLANE_SIZE)
    ]
    for copy in copies:
        copy.start()
    for copy in copies:
        copy.wait()


def push_kernel(side, live_ref, docs_ref, labels_ref, *refs):
    before_ref, out_ref, tasks, select = refs if side else (None, *refs)
    _, zp, zb, _, _, _ = place()
    width = labels_ref.shape[1]
    first = first_blocks()[side]
    lane = lax.broadcasted_iota(jnp.int32, (1, LAB_BLK), 1) ^ (16 * zb)

    row = lax.broadcasted_iota(jnp.int32, select.shape, 0)
    group = lax.broadcasted_iota(jnp.int32, select.shape, 1) // 128
    select[...] = jnp.where(
        row == group, float(LAB_BLK), jnp.where(row == group + POS, 1.0, 0.0)
    ).astype(jnp.bfloat16)

    def listed(which, run):
        column = (run // 4) * 128 + (zp * 2 + zb) * 4 + run % 4
        live = [live_ref[which * 4 + i, column] for i in range(4)]
        low = jnp.where(live[0] > 0, 0, jnp.where(live[1] > 0, 1, jnp.where(live[2] > 0, 2, 3)))
        high = jnp.where(live[3] > 0, 3, jnp.where(live[2] > 0, 2, jnp.where(live[1] > 0, 1, 0)))
        return live[0] + live[1] + live[2] + live[3], low, high

    number = jnp.int32(0)
    for run in range(RUNS):
        count, low, high = listed(side, run)
        begun = listed(0, run)[0] if side else jnp.int32(0)
        for i, value in enumerate((run, low, high, count, begun)):
            tasks[5 * number + i] = value
        number = number + jnp.where(count > 0, 1, 0)
        if side:
            rows = pl.ds(run * RUN, RUN)

            @pl.when((count == 0) & (begun > 0))
            def _():
                out_ref[rows, :] = before_ref[rows, :].astype(out_ref.dtype)

            @pl.when((count == 0) & (begun == 0))
            def _():
                out_ref[rows, :] = jnp.zeros((RUN, width), out_ref.dtype)

    def coefficients(task):
        run, low, high, count, begun = (tasks[5 * task + i] for i in range(5))
        rows = pl.ds(pl.multiple_of(run * RUN, RUN), RUN)
        panel = jnp.concatenate(
            [
                labels_ref[pl.ds(pl.multiple_of(b * LAB_BLK, LAB_BLK), LAB_BLK), :]
                for b in (low, high)
            ],
            axis=0,
        )
        scores = SCALE * lax.dot_general(
            docs_ref[rows, :width],
            panel,
            (((1,), (1,)), ((), ())),
            preferred_element_type=jnp.float32,
        )
        pos_ids = jnp.dot(docs_ref[rows, width:], select[...], preferred_element_type=jnp.float32)
        halves = []
        for i, block in enumerate((low, high)):
            ids = ((first + block) * LAB_BLK + lane).astype(jnp.float32)
            hit = pos_ids[:, :128] == ids
            for k in range(1, POS):
                hit = hit | (pos_ids[:, k * 128 : (k + 1) * 128] == ids)
            sigmoid = jax.nn.sigmoid(scores[:, i * LAB_BLK : (i + 1) * LAB_BLK])
            coef = SCALE * (sigmoid - jnp.where(hit, 1.0, 0.0))
            if i:
                coef = jnp.where(count > 1, coef, 0.0)
            halves.append(coef.astype(jnp.bfloat16))
        return rows, jnp.concatenate(halves, axis=1), panel, begun

    def batch(start, size):
        ready = [coefficients(jnp.minimum(start + i, number - 1)) for i in range(size)]
        for rows, coef, panel, begun in ready:
            for left in range(0, width, 256):
                columns = slice(left, left + 256)
                total = jnp.dot(coef, panel[:, columns], preferred_element_type=jnp.float32)
                if side:
                    total = jnp.where(begun > 0, total + before_ref[rows, columns], total)
                out_ref[rows, columns] = total.astype(out_ref.dtype)

    rest = number % 4

    @pl.loop(0, (number + 1) // 4)
    def _(i):
        batch(4 * i, 4)

    @pl.when((rest == 1) | (rest == 2))
    def _():
        batch(number - rest, 2)


def finish_kernel(pieces_ref, doc_ref, out_ref):
    summed = pieces_ref[0].astype(jnp.float32)
    for i in range(1, PLANE_SIZE):
        summed = summed + pieces_ref[i].astype(jnp.float32)
    own_unit, own_norm = unit_rows(doc_ref[...])
    radial = jnp.sum(summed * own_unit, axis=-1, keepdims=True)
    out_ref[...] = (summed - radial * own_unit) / own_norm


def vmem(count):
    return [pl.BlockSpec(memory_space=pltpu.VMEM)] * count


def body(doc_emb, label_emb, short_blocks, short_len, positives):
    rows, width = doc_emb.shape
    neighbour = lax.ppermute(label_emb, "zb", [(0, 1), (1, 0)])
    spread = pl.pallas_call(
        prepare_kernel,
        out_shape=jax.ShapeDtypeStruct((PLANE_SIZE, rows, width + 128), jnp.bfloat16),
        in_specs=vmem(2),
        out_specs=pl.BlockSpec(memory_space=pl.ANY),
        scratch_shapes=[
            pltpu.VMEM((rows, width + 128), jnp.bfloat16),
            pltpu.SemaphoreType.DMA((PLANE_SIZE,)),
        ],
        cost_estimate=pl.CostEstimate(
            flops=8 * rows * width, bytes_accessed=8 * 2**20, transcendentals=rows
        ),
    )(doc_emb, positives.T)
    docs = lax.all_to_all(spread, PLANE, split_axis=0, concat_axis=0, tiled=True)
    docs = docs.reshape(PLANE_SIZE * rows, width + 128)
    pair = jnp.concatenate([label_emb, neighbour], axis=0)
    pair = unit_rows(pair)[0].astype(jnp.bfloat16)
    own_labels = lax.all_gather(pair, "zp", axis=0, tiled=True)
    other_labels = lax.ppermute(own_labels, "c", [(0, 1), (1, 0)])

    grid = jnp.arange(4, dtype=jnp.int32)
    block_ids = jnp.concatenate([first + grid for first in first_blocks()])
    slot = jnp.arange(short_blocks.shape[1], dtype=jnp.int32)
    live = jnp.any(
        (short_blocks.T[None] == block_ids[:, None, None])
        & (slot[:, None] < short_len[None, :])[None],
        axis=1,
    ).astype(jnp.int32)

    def push(side, dtype, *operands):
        return pl.pallas_call(
            functools.partial(push_kernel, side),
            out_shape=jax.ShapeDtypeStruct((RUNS * RUN, width), dtype),
            in_specs=[pl.BlockSpec(memory_space=pltpu.SMEM)] + vmem(len(operands)),
            out_specs=vmem(1)[0],
            scratch_shapes=[
                pltpu.SMEM((5 * RUNS,), jnp.int32),
                pltpu.VMEM((128, POS * 128), jnp.bfloat16),
            ],
            compiler_params=pltpu.CompilerParams(vmem_limit_bytes=32 * 2**20),
            cost_estimate=pl.CostEstimate(
                flops=4 * RUNS * RUN * 2 * LAB_BLK * width,
                bytes_accessed=6 * 2**20,
                transcendentals=2 * RUNS * RUN * 2 * LAB_BLK,
            ),
        )(live, *operands)

    part = push(0, jnp.float32, docs, own_labels)
    part = push(1, jnp.bfloat16, docs, other_labels, part)
    pieces = lax.all_to_all(
        part.reshape(PLANE_SIZE, rows, width), PLANE, split_axis=0, concat_axis=0, tiled=True
    )
    return pl.pallas_call(
        finish_kernel,
        out_shape=jax.ShapeDtypeStruct((rows, width), jnp.float32),
        in_specs=vmem(2),
        out_specs=vmem(1)[0],
        compiler_params=pltpu.CompilerParams(vmem_limit_bytes=32 * 2**20),
    )(pieces, doc_emb)


def solution(mesh):
    fine = Mesh(mesh.devices.reshape(SIZES), AXES)
    doc, label = AXES[:3], AXES[3:]
    placed = (P(doc + label, None), P(label + doc, None), P(), P(), P(doc, None))
    return jax.shard_map(
        body, mesh=fine, in_specs=placed, out_specs=P(doc + label, None), check_vma=False
    )
```
